32 devices in a mesh: parts: 2 (over y), view: 4 (over z), pix: 4 (over x, core).
Axes of the slice: x: 2, y: 2, z: 4, core: 2. Of those that a mesh axis runs over, the one named last changes fastest.
Arguments:
- descriptors: bfloat16 [8, 768, 256], P(('parts', 'view'), 'pix'), parts along dimension 0, may hold values from -6 to 6
- matches: int32 [8, 4, 768], P(('parts', 'view'), None, 'pix'), parts along dimension 0, may hold values from 0 to 767
Outputs:
- descriptor_grad: bfloat16 [8, 768, 256], P(('parts', 'view'), 'pix'), parts along dimension 0
- pixel_loss: float32 [8, 768], P(('parts', 'view'), 'pix'), parts along dimension 0
The draws below stay inside these ranges and needn't reach their ends.
There are 2 independent parts, one for each index of `parts`. The reference program is written for one: setup_inputs(seed, part) draws one part's arguments, and reference() takes and returns one part's arrays. A program takes and returns all parts, laid end to end along the dimension named above; each array names one. Nothing has to cross between parts.
Inputs may be any that keep to these rules, and one draw needn't show every extreme that they name: `matches`: entries with a == b are not used.
All inputs are finite; a program needn't handle non-finite values.
Results may differ from the reference program's by a relative error of at most 0.0053.
Values may be sent and summed in bfloat16 or wider, within the bound.
A program may use at most 128 MiB of HBM per device.

```python
import math
import jax
import jax.numpy as jnp
from jax import lax

C = 256
VIEWS = 4
PIX = 768


def with_ends(array, key, least, largest):
    shape = array.shape
    index_at = [jax.random.randint(jax.random.fold_in(key, axis), (), 0, shape[axis]) for axis in range(len(shape))]
    array = array.at[tuple(index_at)].set(least)
    longest = shape.index(max(shape))
    index_at[longest] = (index_at[longest] + 1) % shape[longest]
    return array.at[tuple(index_at)].set(largest)


def shard_levels(key, dims, split, least, high):
    loudness = 1.0
    for axis_at, shards_of in split:
        draws = jax.random.uniform(jax.random.fold_in(jax.random.fold_in(key, 6), axis_at), (shards_of,), jnp.float32, least / len(split), high / len(split))
        loudness = loudness * jnp.repeat(jnp.exp(draws), dims[axis_at] // shards_of).reshape((-1,) + (1,) * (len(dims) - 1 - axis_at))
    return loudness


def noise(stream_key, shape, width, bound, pieces=(), kind=jnp.bfloat16):
    drawn = width * jax.random.normal(stream_key, shape, jnp.float32)
    if pieces:
        drawn = drawn * shard_levels(stream_key, shape, pieces, -0.22, 0.18)
    return jnp.clip(drawn, -bound, bound).astype(kind)


def setup_inputs(seed: int = 0, part: int = 0) -> dict:
    streams_of = jax.random.split(jax.random.key(seed), 3)
    own_keys = jax.random.split(jax.random.fold_in(streams_of[2], part), 3)
    descriptors = noise(own_keys[0], (VIEWS, PIX, C), 1.0, 6.0, ((0, 4), (1, 4)))
    matches = with_ends(jax.random.randint(own_keys[1], (VIEWS, VIEWS, PIX), 0, PIX), jax.random.fold_in(own_keys[1], 1), 0, PIX - 1).astype(jnp.int32)
    return dict(descriptors=descriptors, matches=matches)


INV_TEMP = 1.0 / 0.07

def normalize(descriptors):
    raw = descriptors.astype(jnp.float32)
    scale = lax.rsqrt(lax.optimization_barrier(jnp.mean(raw * raw, axis=-1, keepdims=True)) + 1e-06) / math.sqrt(raw.shape[-1])
    unit = raw * scale
    return (scale, unit, unit.astype(jnp.bfloat16))

def reference(descriptors, matches):
    scale, unit, normed = normalize(descriptors)
    column_ids = jnp.arange(PIX, dtype=jnp.int32)

    def weights(first, second, totals):
        sim = INV_TEMP * jnp.dot(normed[first], normed[second].T, preferred_element_type=jnp.float32)
        idx = matches[first, second]
        hits = (column_ids[None, :] == idx[:, None]).astype(jnp.float32)
        wgt = jnp.exp(sim) / totals[:, None] - hits
        wgt = jnp.where(first != second, wgt, 0.0).astype(jnp.bfloat16)
        return (sim, idx, wgt)

    def per_view(first):

        def step(carry, second):
            row_acc, loss_acc = carry
            sim = INV_TEMP * jnp.dot(normed[first], normed[second].T, preferred_element_type=jnp.float32)
            totals = lax.optimization_barrier(jnp.sum(jnp.exp(sim), axis=1))
            idx = matches[first, second]
            pos = jnp.take_along_axis(sim, idx[:, None], axis=1)[:, 0]
            valid = first != second
            loss_acc = loss_acc + jnp.where(valid, jnp.log(totals) - pos, 0.0)
            hits = (column_ids[None, :] == idx[:, None]).astype(jnp.float32)
            wgt = jnp.where(valid, jnp.exp(sim) / totals[:, None] - hits, 0.0).astype(jnp.bfloat16)
            row_acc = row_acc + jnp.dot(wgt, normed[second], preferred_element_type=jnp.float32)
            return ((row_acc, loss_acc), totals)
        init = (jnp.zeros((PIX, C), jnp.float32), jnp.zeros((PIX,), jnp.float32))
        (row_acc, loss_acc), totals = lax.scan(step, init, jnp.arange(VIEWS, dtype=jnp.int32))
        return (row_acc, loss_acc, totals)
    row_term, loss_sum, all_totals = lax.map(per_view, jnp.arange(VIEWS, dtype=jnp.int32))

    def column_view(second):

        def step(acc, first):
            sim, idx, wgt = weights(first, second, all_totals[first, second])
            return (acc + jnp.dot(wgt.T, normed[first], preferred_element_type=jnp.float32), None)
        acc, unused = lax.scan(step, jnp.zeros((PIX, C), jnp.float32), jnp.arange(VIEWS, dtype=jnp.int32))
        return acc
    column_term = lax.map(column_view, jnp.arange(VIEWS, dtype=jnp.int32))
    unit_grad = INV_TEMP / (VIEWS - 1) * (row_term + column_term)
    along = lax.optimization_barrier(jnp.sum(unit * unit_grad, axis=-1, keepdims=True))
    descriptor_grad = (scale * (unit_grad - unit * along)).astype(jnp.bfloat16)
    pixel_loss = loss_sum / (VIEWS - 1)
    return (descriptor_grad, pixel_loss)
```

```python
import functools
import math

import jax
import jax.numpy as jnp
from jax import lax
from jax.experimental import pallas as pl
from jax.experimental.pallas import tpu as pltpu
from jax.sharding import PartitionSpec as P

MESH = pl.DeviceIdType.MESH
INV_TEMP = 1.0 / 0.07
LOG2E = math.log2(math.e)
UP, DOWN, RIGHT, LEFT, TWIN = range(5)


def kernel(
    views, slots, desc_ref, match_ref, grad_ref, loss_ref, held, acc, loss, send_sem, recv_sem
):
    rows, width = desc_ref.shape
    chips = slots // 2
    extra = held.shape[2] - rows
    v = lax.axis_index("view")
    p = lax.axis_index("pix")
    x, c = p // 2, lax.rem(p, 2)
    there = {
        UP: (v + 1 < views, {"view": v + 1}),
        DOWN: (v >= 1, {"view": v - 1}),
        RIGHT: (x + 1 < chips, {"pix": p + 2}),
        LEFT: (x >= 1, {"pix": p - 2}),
        TWIN: (c >= 0, {"pix": p + 1 - 2 * c}),
    }

    barrier = pltpu.get_barrier_semaphore()
    count = 0
    for way in there:
        exists, target = there[way]

        @pl.when(exists)
        def _():
            pl.semaphore_signal(barrier, inc=1, device_id=target, device_id_type=MESH)

        count = count + exists.astype(jnp.int32)

    raw = desc_ref[...].astype(jnp.float32)
    scale = lax.rsqrt(jnp.mean(raw * raw, axis=-1, keepdims=True) + 1e-06) / math.sqrt(width)
    unit = raw * scale
    held[v, p, :rows, :] = unit.astype(jnp.bfloat16)
    own_links = match_ref[...]
    high = own_links // 256
    low = own_links - 256 * high
    links = jnp.concatenate([high, low], axis=0).astype(jnp.float32)
    links = jnp.concatenate([links, jnp.zeros((2 * views, width - rows), jnp.float32)], axis=1)
    if extra > 2 * views:
        links = jnp.concatenate([links, jnp.zeros((extra - 2 * views, width), jnp.float32)], axis=0)
    held[v, p, rows:, :] = links.astype(jnp.bfloat16)
    acc[...] = jnp.zeros_like(acc)
    loss[...] = jnp.zeros_like(loss)
    pl.semaphore_wait(barrier, count)

    def copy(way, view, slot):
        return pltpu.make_async_remote_copy(
            src_ref=held.at[view, slot],
            dst_ref=held.at[view, slot],
            send_sem=send_sem.at[way, view, slot],
            recv_sem=recv_sem.at[view, slot],
            device_id=there[way][1],
            device_id_type=MESH,
        )

    def send(way, view, slot):
        @pl.when(there[way][0])
        def _():
            copy(way, view, slot).start()

    def arrive(view, slot):
        copy(TWIN, view, slot).wait_recv()

    for way in (UP, DOWN, RIGHT, LEFT, TWIN):
        send(way, v, p)
    for step in range(1, chips):
        for sign, way in ((-1, RIGHT), (1, LEFT)):
            origin = x + sign * step

            @pl.when((origin >= 0) & (origin < chips))
            def _():
                slot = 2 * origin + c
                arrive(v, slot)
                for onward in (UP, DOWN, way, TWIN):
                    send(onward, v, slot)

    def forward(step):
        for q in range(chips):
            slot = 2 * q + c
            for sign, way in ((-1, UP), (1, DOWN)):
                view = v + sign * step

                @pl.when((view >= 0) & (view < views))
                def _():
                    arrive(view, slot)
                    send(way, view, slot)
                    send(TWIN, view, slot)

    def whole(view):
        return held[view, :, :rows, :].reshape(slots * rows, width)

    def exponent(left, right):
        dots = lax.dot_general(
            left, right, (((1,), (1,)), ((), ())), preferred_element_type=jnp.float32
        )
        return dots * (INV_TEMP * LOG2E)

    eye = lax.broadcasted_iota(jnp.int32, (rows, rows), 0) == lax.broadcasted_iota(
        jnp.int32, (rows, rows), 1
    )

    def compute(view):
        for q in range(chips):
            arrive(view, 2 * q + 1 - c)
        right = whole(view)
        power = exponent(held[v, p, :rows, :], right)
        expo = jnp.exp2(power)
        row_total = jnp.sum(expo, axis=1, keepdims=True)
        mine = match_ref[pl.ds(view, 1), :]
        mine = jnp.sum(jnp.where(eye, mine, 0).astype(jnp.float32), axis=1, keepdims=True)
        ids = lax.broadcasted_iota(jnp.int32, expo.shape, 1).astype(jnp.float32)
        row_hit = ids == mine
        positive = jnp.sum(jnp.where(row_hit, power, 0.0), axis=1, keepdims=True)
        loss[...] += jnp.log(row_total) - (1.0 / LOG2E) * positive

        def add(k, total):
            other = held[v, lax.rem(p + k, slots), :rows, :]
            return total + jnp.sum(
                jnp.exp2(exponent(other, right)), axis=0, keepdims=True
            )

        col_total = lax.fori_loop(1, slots, add, jnp.sum(expo, axis=0, keepdims=True))
        at = lax.broadcasted_iota(jnp.int32, (extra, width), 0)
        digit = jnp.where(at == v, 256.0, jnp.where(at == v + views, 1.0, 0.0))
        theirs = [
            jnp.sum(digit * held[view, s, rows:, :].astype(jnp.float32), axis=0, keepdims=True)[
                :, :rows
            ]
            for s in range(slots)
        ]
        theirs = jnp.concatenate(theirs, axis=1)
        own_ids = (lax.broadcasted_iota(jnp.int32, expo.shape, 0) + p * rows).astype(jnp.float32)
        col_hit = own_ids == theirs
        weight = expo * (1.0 / row_total + 1.0 / col_total)
        weight = weight - jnp.where(row_hit, 1.0, 0.0) - jnp.where(col_hit, 1.0, 0.0)
        acc[...] += jnp.dot(
            weight.astype(jnp.bfloat16), right, preferred_element_type=jnp.float32
        )

    def both(step):
        def one(k, carry):
            view = v + step * (2 * k - 1)

            @pl.when((view >= 0) & (view < views))
            def _():
                compute(view)

            return carry

        lax.fori_loop(0, 2, one, 0)

    def round_of(step, carry):
        @pl.when(step < views)
        def _():
            forward(step)

        @pl.when(step == 1)
        def _():
            for q in range(chips):
                arrive(v, 2 * q + 1 - c)

        @pl.when(step >= 2)
        def _():
            both(step - 1)

        return carry

    lax.fori_loop(1, views + 1, round_of, 0)

    unit_grad = (INV_TEMP / (views - 1)) * acc[...]
    raw = desc_ref[...].astype(jnp.float32)
    scale = lax.rsqrt(jnp.mean(raw * raw, axis=-1, keepdims=True) + 1e-06) / math.sqrt(width)
    unit = raw * scale
    along = jnp.sum(unit * unit_grad, axis=-1, keepdims=True)
    grad_ref[...] = (scale * (unit_grad - unit * along)).astype(jnp.bfloat16)
    loss_ref[...] = jnp.sum(
        jnp.where(eye, loss[...] * (1.0 / (views - 1)), 0.0), axis=0, keepdims=True
    )

    def sent(way, view, slot):
        @pl.when(there[way][0])
        def _():
            copy(way, view, slot).wait_send()

    def drain(view, carry):
        for q in range(chips):
            slot = 2 * q + c
            sent(TWIN, view, slot)

            @pl.when(view <= v)
            def _():
                sent(UP, view, slot)

            @pl.when(view >= v)
            def _():
                sent(DOWN, view, slot)

        return carry

    lax.fori_loop(0, views, drain, 0)
    for q in range(chips):

        @pl.when(q <= x)
        def _():
            sent(RIGHT, v, 2 * q + c)

        @pl.when(q >= x)
        def _():
            sent(LEFT, v, 2 * q + c)


def body(views, slots, descriptors, matches):
    rows, width = descriptors.shape[1:]
    extra = -(-2 * views // 16) * 16
    grad, loss = pl.pallas_call(
        functools.partial(kernel, views, slots),
        out_shape=(
            jax.ShapeDtypeStruct((rows, width), jnp.bfloat16),
            jax.ShapeDtypeStruct((1, rows), jnp.float32),
        ),
        in_specs=[pl.BlockSpec(memory_space=pltpu.VMEM)] * 2,
        out_specs=(pl.BlockSpec(memory_space=pltpu.VMEM),) * 2,
        scratch_shapes=[
            pltpu.VMEM((views, slots, rows + extra, width), jnp.bfloat16),
            pltpu.VMEM((rows, width), jnp.float32),
            pltpu.VMEM((rows, 1), jnp.float32),
            pltpu.SemaphoreType.DMA((5, views, slots)),
            pltpu.SemaphoreType.DMA((views, slots)),
        ],
        compiler_params=pltpu.CompilerParams(
            collective_id=0, has_side_effects=True, vmem_limit_bytes=48 * 1024 * 1024
        ),
        cost_estimate=pl.CostEstimate(
            flops=2 * (slots + 1) * rows * (views - 1) * slots * rows * width,
            bytes_accessed=4 * rows * width,
            transcendentals=slots * rows * (views - 1) * slots * rows,
        ),
    )(descriptors[0], matches[0])
    return grad[None], loss


def solution(mesh):
    views, slots = mesh.shape["view"], mesh.shape["pix"]
    in_specs = (P(("parts", "view"), "pix", None), P(("parts", "view"), None, "pix"))
    out_specs = (P(("parts", "view"), "pix", None), P(("parts", "view"), "pix"))
    return jax.shard_map(
        functools.partial(body, views, slots),
        mesh=mesh, in_specs=in_specs, out_specs=out_specs, check_vma=False,
    )
```

```python
import functools
import math

import jax
import jax.numpy as jnp
from jax import lax
from jax.experimental import pallas as pl
from jax.experimental.pallas import tpu as pltpu
from jax.sharding import PartitionSpec as P

MESH = pl.DeviceIdType.MESH
INV_TEMP = 1.0 / 0.07
LOG2E = math.log2(math.e)
CHUNKS = 1
UP, DOWN, RIGHT, LEFT, TWIN = range(5)


def kernel(
    views, slots, desc_any, match_any, grad_ref, loss_ref,
    desc_ref, match_ref, held, acc, loss, expos, rest, row_total, load_sem, send_sem, recv_sem,
):
    loads = [
        pltpu.make_async_copy(desc_any, desc_ref, load_sem.at[0]),
        pltpu.make_async_copy(match_any, match_ref, load_sem.at[1]),
    ]
    for load in loads:
        load.start()
    rows, width = desc_ref.shape
    chips = slots // 2
    extra = held.shape[2] - rows
    tiles = (rows + extra) // 16
    cuts = [16 * (tiles * k // CHUNKS) for k in range(CHUNKS + 1)]
    v = lax.axis_index("view")
    p = lax.axis_index("pix")
    x, c = p // 2, lax.rem(p, 2)
    there = {
        UP: (v + 1 < views, {"view": v + 1}),
        DOWN: (v >= 1, {"view": v - 1}),
        RIGHT: (x + 1 < chips, {"pix": p + 2}),
        LEFT: (x >= 1, {"pix": p - 2}),
        TWIN: (c >= 0, {"pix": p + 1 - 2 * c}),
    }

    barrier = pltpu.get_barrier_semaphore()
    count = 0
    for way in there:
        exists, target = there[way]

        @pl.when(exists)
        def _():
            pl.semaphore_signal(barrier, inc=1, device_id=target, device_id_type=MESH)

        count = count + exists.astype(jnp.int32)

    for load in loads:
        load.wait()
    raw = desc_ref[...].astype(jnp.float32)
    scale = lax.rsqrt(jnp.mean(raw * raw, axis=-1, keepdims=True) + 1e-06) / math.sqrt(width)
    unit = raw * scale
    held[v, p, :rows, :] = unit.astype(jnp.bfloat16)
    own_links = match_ref[...]
    high = own_links // 256
    low = own_links - 256 * high
    links = jnp.concatenate([high, low], axis=0).astype(jnp.float32)
    links = jnp.concatenate([links, jnp.zeros((2 * views, width - rows), jnp.float32)], axis=1)
    if extra > 2 * views:
        links = jnp.concatenate([links, jnp.zeros((extra - 2 * views, width), jnp.float32)], axis=0)
    held[v, p, rows:, :] = links.astype(jnp.bfloat16)
    acc[...] = jnp.zeros_like(acc)
    loss[...] = jnp.zeros_like(loss)
    pl.semaphore_wait(barrier, count)

    def piece(view, slot, k):
        return held.at[view, slot, pl.ds(cuts[k], cuts[k + 1] - cuts[k])]

    def copy(way, view, slot, k):
        return pltpu.make_async_remote_copy(
            src_ref=piece(view, slot, k),
            dst_ref=piece(view, slot, k),
            send_sem=send_sem.at[way, view, slot, k],
            recv_sem=recv_sem.at[view, slot, k],
            device_id=there[way][1],
            device_id_type=MESH,
        )

    def send(way, view, slot, k):
        @pl.when(there[way][0])
        def _():
            copy(way, view, slot, k).start()

    def arrive(view, slot, k):
        copy(TWIN, view, slot, k).wait_recv()

    def sides(step, act):
        for sign, onward in ((-1, UP), (1, DOWN)):
            view = v + sign * step

            @pl.when((view >= 0) & (view < views))
            def _():
                act(view, onward)

    for k in range(CHUNKS):
        for way in (UP, DOWN, RIGHT, LEFT, TWIN):
            send(way, v, p, k)

    def along_view(step):
        def act(view, onward):
            for k in range(CHUNKS):
                arrive(view, p, k)
                for way in (onward, RIGHT, LEFT, TWIN):
                    send(way, view, p, k)

        sides(step, act)

    def along_x(view):
        for step in range(1, chips):
            for sign, way in ((-1, RIGHT), (1, LEFT)):
                origin = x + sign * step

                @pl.when((origin >= 0) & (origin < chips))
                def _():
                    slot = 2 * origin + c
                    for k in range(CHUNKS):
                        arrive(view, slot, k)
                        send(way, view, slot, k)
                        send(TWIN, view, slot, k)

    def from_twin(view, q):
        for k in range(CHUNKS):
            arrive(view, 2 * q + 1 - c, k)

    def pair(view, q):
        return held[view, pl.ds(2 * q, 2), :rows, :].reshape(2 * rows, width)

    def exponent(left, right):
        dots = lax.dot_general(
            left, right, (((1,), (1,)), ((), ())), preferred_element_type=jnp.float32
        )
        return dots * (INV_TEMP * LOG2E)

    eye = lax.broadcasted_iota(jnp.int32, (rows, rows), 0) == lax.broadcasted_iota(
        jnp.int32, (rows, rows), 1
    )

    def half(view, place, q):
        from_twin(view, q)
        right = pair(view, q)
        power = exponent(held[v, p, :rows, :], right)
        expo = jnp.exp2(power)
        row_total[place] += jnp.sum(expo, axis=1, keepdims=True)
        mine = match_ref[pl.ds(view, 1), :]
        mine = jnp.sum(jnp.where(eye, mine, 0).astype(jnp.float32), axis=1, keepdims=True)
        first = (2 * q * rows).astype(jnp.float32)
        ids = lax.broadcasted_iota(jnp.int32, expo.shape, 1).astype(jnp.float32) + first
        row_hit = ids == mine
        loss[...] -= (1.0 / LOG2E) * jnp.sum(
            jnp.where(row_hit, power, 0.0), axis=1, keepdims=True
        )

        def add(k, total):
            other = held[v, lax.rem(p + k, slots), :rows, :]
            return total + jnp.sum(jnp.exp2(exponent(other, right)), axis=0, keepdims=True)

        col_total = lax.fori_loop(
            1, slots, add, jnp.sum(expo, axis=0, keepdims=True), unroll=slots <= 4
        )
        at = lax.broadcasted_iota(jnp.int32, (extra, width), 0)
        digit = jnp.where(at == v, 256.0, jnp.where(at == v + views, 1.0, 0.0))
        theirs = [
            jnp.sum(
                digit * held[view, 2 * q + s, rows:, :].astype(jnp.float32), axis=0, keepdims=True
            )[:, :rows]
            for s in range(2)
        ]
        theirs = jnp.concatenate(theirs, axis=1)
        own_ids = (lax.broadcasted_iota(jnp.int32, expo.shape, 0) + p * rows).astype(jnp.float32)
        col_hit = own_ids == theirs
        expos[place, q] = expo
        rest[place, q] = (
            expo * (1.0 / col_total) - jnp.where(row_hit, 1.0, 0.0) - jnp.where(col_hit, 1.0, 0.0)
        )

    def finish(view, place):
        total = row_total[place]
        row_total[place] = jnp.zeros_like(total)
        loss[...] += jnp.log(total)
        inverse = 1.0 / total

        def one(q, carry):
            weight = expos[place, q] * inverse + rest[place, q]
            acc[...] += jnp.dot(
                weight.astype(jnp.bfloat16), pair(view, q), preferred_element_type=jnp.float32
            )
            return carry

        lax.fori_loop(0, chips, one, 0, unroll=chips <= 2)

    row_total[...] = jnp.zeros_like(row_total)

    def round_of(step, carry):
        @pl.when(step < views)
        def _():
            along_view(step)

        @pl.when(step == 1)
        def _():
            along_x(v)
            for q in range(chips):
                from_twin(v, q)

        @pl.when(step > 1)
        def _():
            sides(step - 1, lambda view, onward: along_x(view))

        def work(k, carry):
            late = (k // 2) == 0
            away = jnp.where(late, step - 1, step)
            side = lax.rem(k, 2)
            view = v + away * (2 * side - 1)
            place = 2 * lax.rem(away, 2) + side
            fine = (view >= 0) & (view < views) & (away >= 1) & (away < views)

            def part(n, carry):
                half(view, place, lax.rem(x + n, chips))
                return carry

            @pl.when(fine)
            def _():
                lax.fori_loop(jnp.where(late, 1, 0), jnp.where(late, chips, 1), part, 0)

            @pl.when(fine & late)
            def _():
                finish(view, place)

            return carry

        lax.fori_loop(0, 4, work, 0)
        return carry

    lax.fori_loop(1, views + 1, round_of, 0)

    unit_grad = (INV_TEMP / (views - 1)) * acc[...]
    raw = desc_ref[...].astype(jnp.float32)
    scale = lax.rsqrt(jnp.mean(raw * raw, axis=-1, keepdims=True) + 1e-06) / math.sqrt(width)
    unit = raw * scale
    along = jnp.sum(unit * unit_grad, axis=-1, keepdims=True)
    grad_ref[...] = (scale * (unit_grad - unit * along)).astype(jnp.bfloat16)
    loss_ref[...] = jnp.sum(
        jnp.where(eye, loss[...] * (1.0 / (views - 1)), 0.0), axis=0, keepdims=True
    )

    def sent(way, view, slot):
        @pl.when(there[way][0])
        def _():
            for k in range(CHUNKS):
                copy(way, view, slot, k).wait_send()

    def drain(view, carry):
        @pl.when(view <= v)
        def _():
            sent(UP, view, p)

        @pl.when(view >= v)
        def _():
            sent(DOWN, view, p)

        for q in range(chips):
            slot = 2 * q + c
            sent(TWIN, view, slot)

            @pl.when(q <= x)
            def _():
                sent(RIGHT, view, slot)

            @pl.when(q >= x)
            def _():
                sent(LEFT, view, slot)

        return carry

    lax.fori_loop(0, views, drain, 0)


def body(views, slots, descriptors, matches):
    rows, width = descriptors.shape[1:]
    extra = -(-2 * views // 16) * 16
    grad, loss = pl.pallas_call(
        functools.partial(kernel, views, slots),
        out_shape=(
            jax.ShapeDtypeStruct((rows, width), jnp.bfloat16),
            jax.ShapeDtypeStruct((1, rows), jnp.float32),
        ),
        in_specs=[pl.BlockSpec(memory_space=pl.ANY)] * 2,
        out_specs=(pl.BlockSpec(memory_space=pltpu.VMEM),) * 2,
        scratch_shapes=[
            pltpu.VMEM((rows, width), jnp.bfloat16),
            pltpu.VMEM((views, rows), jnp.int32),
            pltpu.VMEM((views, slots, rows + extra, width), jnp.bfloat16),
            pltpu.VMEM((rows, width), jnp.float32),
            pltpu.VMEM((rows, 1), jnp.float32),
            pltpu.VMEM((4, slots // 2, rows, 2 * rows), jnp.float32),
            pltpu.VMEM((4, slots // 2, rows, 2 * rows), jnp.float32),
            pltpu.VMEM((4, rows, 1), jnp.float32),
            pltpu.SemaphoreType.DMA((2,)),
            pltpu.SemaphoreType.DMA((5, views, slots, CHUNKS)),
            pltpu.SemaphoreType.DMA((views, slots, CHUNKS)),
        ],
        compiler_params=pltpu.CompilerParams(
            collective_id=0, has_side_effects=True, vmem_limit_bytes=48 * 1024 * 1024
        ),
        cost_estimate=pl.CostEstimate(
            flops=2 * (slots + 1) * rows * (views - 1) * slots * rows * width,
            bytes_accessed=4 * rows * width,
            transcendentals=slots * rows * (views - 1) * slots * rows,
        ),
    )(descriptors[0], matches[0])
    return grad[None], loss


def solution(mesh):
    views, slots = mesh.shape["view"], mesh.shape["pix"]
    in_specs = (P(("parts", "view"), "pix", None), P(("parts", "view"), None, "pix"))
    out_specs = (P(("parts", "view"), "pix", None), P(("parts", "view"), "pix"))
    return jax.shard_map(
        functools.partial(body, views, slots),
        mesh=mesh, in_specs=in_specs, out_specs=out_specs, check_vma=False,
    )
```

```python
import functools
import math

import jax
import jax.numpy as jnp
from jax import lax
from jax.experimental import pallas as pl
from jax.experimental.pallas import tpu as pltpu
from jax.sharding import PartitionSpec as P

MESH = pl.DeviceIdType.MESH
INV_TEMP = 1.0 / 0.07
LOG2E = math.log2(math.e)
CHUNKS = 1
UP, DOWN, RIGHT, LEFT, TWIN = range(5)


def kernel(
    views, slots, desc_ref, match_ref, grad_ref, loss_ref,
    held, acc, loss, expos, rest, row_total, send_sem, recv_sem,
):
    rows, width = desc_ref.shape
    chips = slots // 2
    extra = held.shape[2] - rows
    tiles = (rows + extra) // 16
    cuts = [16 * (tiles * k // CHUNKS) for k in range(CHUNKS + 1)]
    v = lax.axis_index("view")
    p = lax.axis_index("pix")
    x, c = p // 2, lax.rem(p, 2)
    there = {
        UP: (v + 1 < views, {"view": v + 1}),
        DOWN: (v >= 1, {"view": v - 1}),
        RIGHT: (x + 1 < chips, {"pix": p + 2}),
        LEFT: (x >= 1, {"pix": p - 2}),
        TWIN: (c >= 0, {"pix": p + 1 - 2 * c}),
    }

    barrier = pltpu.get_barrier_semaphore()
    count = 0
    for way in there:
        exists, target = there[way]

        @pl.when(exists)
        def _():
            pl.semaphore_signal(barrier, inc=1, device_id=target, device_id_type=MESH)

        count = count + exists.astype(jnp.int32)

    raw = desc_ref[...].astype(jnp.float32)
    scale = lax.rsqrt(jnp.mean(raw * raw, axis=-1, keepdims=True) + 1e-06) / math.sqrt(width)
    unit = raw * scale
    held[v, p, :rows, :] = unit.astype(jnp.bfloat16)
    own_links = match_ref[...]
    high = own_links // 256
    low = own_links - 256 * high
    links = jnp.concatenate([high, low], axis=0).astype(jnp.float32)
    links = jnp.concatenate([links, jnp.zeros((2 * views, width - rows), jnp.float32)], axis=1)
    if extra > 2 * views:
        links = jnp.concatenate([links, jnp.zeros((extra - 2 * views, width), jnp.float32)], axis=0)
    held[v, p, rows:, :] = links.astype(jnp.bfloat16)
    acc[...] = jnp.zeros_like(acc)
    loss[...] = jnp.zeros_like(loss)
    pl.semaphore_wait(barrier, count)

    def piece(view, slot, k):
        return held.at[view, slot, pl.ds(cuts[k], cuts[k + 1] - cuts[k])]

    def copy(way, view, slot, k):
        return pltpu.make_async_remote_copy(
            src_ref=piece(view, slot, k),
            dst_ref=piece(view, slot, k),
            send_sem=send_sem.at[way, view, slot, k],
            recv_sem=recv_sem.at[view, slot, k],
            device_id=there[way][1],
            device_id_type=MESH,
        )

    def send(way, view, slot, k):
        @pl.when(there[way][0])
        def _():
            copy(way, view, slot, k).start()

    def arrive(view, slot, k):
        copy(TWIN, view, slot, k).wait_recv()

    def sides(step, act):
        for sign, onward in ((-1, UP), (1, DOWN)):
            view = v + sign * step

            @pl.when((view >= 0) & (view < views))
            def _():
                act(view, onward)

    for k in range(CHUNKS):
        for way in (UP, DOWN, RIGHT, LEFT, TWIN):
            send(way, v, p, k)

    def along_view(step):
        def act(view, onward):
            for k in range(CHUNKS):
                arrive(view, p, k)
                for way in (onward, RIGHT, LEFT, TWIN):
                    send(way, view, p, k)

        sides(step, act)

    def along_x(view):
        for step in range(1, chips):
            for sign, way in ((-1, RIGHT), (1, LEFT)):
                origin = x + sign * step

                @pl.when((origin >= 0) & (origin < chips))
                def _():
                    slot = 2 * origin + c
                    for k in range(CHUNKS):
                        arrive(view, slot, k)
                        send(way, view, slot, k)
                        send(TWIN, view, slot, k)

    def from_twin(view, q):
        for k in range(CHUNKS):
            arrive(view, 2 * q + 1 - c, k)

    def pair(view, q):
        return held[view, pl.ds(2 * q, 2), :rows, :].reshape(2 * rows, width)

    def exponent(left, right):
        dots = lax.dot_general(
            left, right, (((1,), (1,)), ((), ())), preferred_element_type=jnp.float32
        )
        return dots * (INV_TEMP * LOG2E)

    eye = lax.broadcasted_iota(jnp.int32, (rows, rows), 0) == lax.broadcasted_iota(
        jnp.int32, (rows, rows), 1
    )

    def half(view, place, q):
        from_twin(view, q)
        right = pair(view, q)
        power = exponent(held[v, p, :rows, :], right)
        expo = jnp.exp2(power)
        row_total[place] += jnp.sum(expo, axis=1, keepdims=True)
        mine = match_ref[pl.ds(view, 1), :]
        mine = jnp.sum(jnp.where(eye, mine, 0).astype(jnp.float32), axis=1, keepdims=True)
        first = (2 * q * rows).astype(jnp.float32)
        ids = lax.broadcasted_iota(jnp.int32, expo.shape, 1).astype(jnp.float32) + first
        row_hit = ids == mine
        loss[...] -= (1.0 / LOG2E) * jnp.sum(
            jnp.where(row_hit, power, 0.0), axis=1, keepdims=True
        )

        def add(k, total):
            other = held[v, lax.rem(p + k, slots), :rows, :]
            return total + jnp.sum(jnp.exp2(exponent(other, right)), axis=0, keepdims=True)

        col_total = lax.fori_loop(
            1, slots, add, jnp.sum(expo, axis=0, keepdims=True), unroll=slots <= 4
        )
        at = lax.broadcasted_iota(jnp.int32, (extra, width), 0)
        digit = jnp.where(at == v, 256.0, jnp.where(at == v + views, 1.0, 0.0))
        theirs = [
            jnp.sum(
                digit * held[view, 2 * q + s, rows:, :].astype(jnp.float32), axis=0, keepdims=True
            )[:, :rows]
            for s in range(2)
        ]
        theirs = jnp.concatenate(theirs, axis=1)
        own_ids = (lax.broadcasted_iota(jnp.int32, expo.shape, 0) + p * rows).astype(jnp.float32)
        col_hit = own_ids == theirs
        expos[place, q] = expo
        rest[place, q] = (
            expo * (1.0 / col_total) - jnp.where(row_hit, 1.0, 0.0) - jnp.where(col_hit, 1.0, 0.0)
        )

    def finish(view, place):
        total = row_total[place]
        row_total[place] = jnp.zeros_like(total)
        loss[...] += jnp.log(total)
        inverse = 1.0 / total

        def one(q, carry):
            weight = expos[place, q] * inverse + rest[place, q]
            acc[...] += jnp.dot(
                weight.astype(jnp.bfloat16), pair(view, q), preferred_element_type=jnp.float32
            )
            return carry

        lax.fori_loop(0, chips, one, 0, unroll=chips <= 2)

    row_total[...] = jnp.zeros_like(row_total)

    def round_of(step, carry):
        @pl.when(step < views)
        def _():
            along_view(step)

        @pl.when(step == 1)
        def _():
            along_x(v)
            for q in range(chips):
                from_twin(v, q)

        @pl.when(step > 1)
        def _():
            sides(step - 1, lambda view, onward: along_x(view))

        def work(k, carry):
            late = (k // 2) == 0
            away = jnp.where(late, step - 1, step)
            side = lax.rem(k, 2)
            view = v + away * (2 * side - 1)
            place = 2 * lax.rem(away, 2) + side
            fine = (view >= 0) & (view < views) & (away >= 1) & (away < views)

            def part(n, carry):
                half(view, place, lax.rem(x + n, chips))
                return carry

            @pl.when(fine)
            def _():
                lax.fori_loop(jnp.where(late, 1, 0), jnp.where(late, chips, 1), part, 0)

            @pl.when(fine & late)
            def _():
                finish(view, place)

            return carry

        lax.fori_loop(0, 4, work, 0)
        return carry

    lax.fori_loop(1, views + 1, round_of, 0)

    unit_grad = (INV_TEMP / (views - 1)) * acc[...]
    raw = desc_ref[...].astype(jnp.float32)
    scale = lax.rsqrt(jnp.mean(raw * raw, axis=-1, keepdims=True) + 1e-06) / math.sqrt(width)
    unit = raw * scale
    along = jnp.sum(unit * unit_grad, axis=-1, keepdims=True)
    grad_ref[...] = (scale * (unit_grad - unit * along)).astype(jnp.bfloat16)
    loss_ref[...] = jnp.sum(
        jnp.where(eye, loss[...] * (1.0 / (views - 1)), 0.0), axis=0, keepdims=True
    )

    def sent(way, view, slot):
        @pl.when(there[way][0])
        def _():
            for k in range(CHUNKS):
                copy(way, view, slot, k).wait_send()

    def drain(view, carry):
        @pl.when(view <= v)
        def _():
            sent(UP, view, p)

        @pl.when(view >= v)
        def _():
            sent(DOWN, view, p)

        for q in range(chips):
            slot = 2 * q + c
            sent(TWIN, view, slot)

            @pl.when(q <= x)
            def _():
                sent(RIGHT, view, slot)

            @pl.when(q >= x)
            def _():
                sent(LEFT, view, slot)

        return carry

    lax.fori_loop(0, views, drain, 0)


def body(views, slots, descriptors, matches):
    rows, width = descriptors.shape[1:]
    extra = -(-2 * views // 16) * 16
    grad, loss = pl.pallas_call(
        functools.partial(kernel, views, slots),
        out_shape=(
            jax.ShapeDtypeStruct((rows, width), jnp.bfloat16),
            jax.ShapeDtypeStruct((1, rows), jnp.float32),
        ),
        in_specs=[pl.BlockSpec(memory_space=pltpu.VMEM)] * 2,
        out_specs=(pl.BlockSpec(memory_space=pltpu.VMEM),) * 2,
        scratch_shapes=[
            pltpu.VMEM((views, slots, rows + extra, width), jnp.bfloat16),
            pltpu.VMEM((rows, width), jnp.float32),
            pltpu.VMEM((rows, 1), jnp.float32),
            pltpu.VMEM((4, slots // 2, rows, 2 * rows), jnp.float32),
            pltpu.VMEM((4, slots // 2, rows, 2 * rows), jnp.float32),
            pltpu.VMEM((4, rows, 1), jnp.float32),
            pltpu.SemaphoreType.DMA((5, views, slots, CHUNKS)),
            pltpu.SemaphoreType.DMA((views, slots, CHUNKS)),
        ],
        compiler_params=pltpu.CompilerParams(
            collective_id=0, has_side_effects=True, vmem_limit_bytes=48 * 1024 * 1024
        ),
        cost_estimate=pl.CostEstimate(
            flops=2 * (slots + 1) * rows * (views - 1) * slots * rows * width,
            bytes_accessed=4 * rows * width,
            transcendentals=slots * rows * (views - 1) * slots * rows,
        ),
    )(descriptors[0], matches[0])
    return grad[None], loss


def solution(mesh):
    views, slots = mesh.shape["view"], mesh.shape["pix"]
    in_specs = (P(("parts", "view"), "pix", None), P(("parts", "view"), None, "pix"))
    out_specs = (P(("parts", "view"), "pix", None), P(("parts", "view"), "pix"))
    return jax.shard_map(
        functools.partial(body, views, slots),
        mesh=mesh, in_specs=in_specs, out_specs=out_specs, check_vma=False,
    )
```

```python
import functools
import math

import jax
import jax.numpy as jnp
from jax import lax
from jax.experimental import pallas as pl
from jax.experimental.pallas import tpu as pltpu
from jax.sharding import PartitionSpec as P

MESH = pl.DeviceIdType.MESH
INV_TEMP = 1.0 / 0.07
LOG2E = math.log2(math.e)
CHUNKS = 1
UP, DOWN, RIGHT, LEFT, TWIN = range(5)


def kernel(
    views, slots, desc_any, match_any, grad_ref, loss_ref,
    desc_ref, match_ref, held, acc, loss, expos, rest, row_total, load_sem, send_sem, recv_sem,
):
    loads = [
        pltpu.make_async_copy(desc_any, desc_ref, load_sem.at[0]),
        pltpu.make_async_copy(match_any, match_ref, load_sem.at[1]),
    ]
    for load in loads:
        load.start()
    rows, width = desc_ref.shape
    chips = slots // 2
    extra = held.shape[2] - rows
    tiles = (rows + extra) // 16
    cuts = [16 * (tiles * k // CHUNKS) for k in range(CHUNKS + 1)]
    v = lax.axis_index("view")
    p = lax.axis_index("pix")
    x, c = p // 2, lax.rem(p, 2)
    there = {
        UP: (v + 1 < views, {"view": v + 1}),
        DOWN: (v >= 1, {"view": v - 1}),
        RIGHT: (x + 1 < chips, {"pix": p + 2}),
        LEFT: (x >= 1, {"pix": p - 2}),
        TWIN: (c >= 0, {"pix": p + 1 - 2 * c}),
    }

    barrier = pltpu.get_barrier_semaphore()
    count = 0
    for way in there:
        exists, target = there[way]

        @pl.when(exists)
        def _():
            pl.semaphore_signal(barrier, inc=1, device_id=target, device_id_type=MESH)

        count = count + exists.astype(jnp.int32)

    for load in loads:
        load.wait()
    raw = desc_ref[...].astype(jnp.float32)
    scale = lax.rsqrt(jnp.mean(raw * raw, axis=-1, keepdims=True) + 1e-06) / math.sqrt(width)
    unit = raw * scale
    held[v, p, :rows, :] = unit.astype(jnp.bfloat16)
    own_links = match_ref[...]
    high = own_links // 256
    low = own_links - 256 * high
    links = jnp.concatenate([high, low], axis=0).astype(jnp.float32)
    links = jnp.concatenate([links, jnp.zeros((2 * views, width - rows), jnp.float32)], axis=1)
    if extra > 2 * views:
        links = jnp.concatenate([links, jnp.zeros((extra - 2 * views, width), jnp.float32)], axis=0)
    held[v, p, rows:, :] = links.astype(jnp.bfloat16)
    acc[...] = jnp.zeros_like(acc)
    loss[...] = jnp.zeros_like(loss)
    pl.semaphore_wait(barrier, count)

    def piece(view, slot, k):
        return held.at[view, slot, pl.ds(cuts[k], cuts[k + 1] - cuts[k])]

    def copy(way, view, slot, k):
        return pltpu.make_async_remote_copy(
            src_ref=piece(view, slot, k),
            dst_ref=piece(view, slot, k),
            send_sem=send_sem.at[way, view, slot, k],
            recv_sem=recv_sem.at[view, slot, k],
            device_id=there[way][1],
            device_id_type=MESH,
        )

    def send(way, view, slot, k):
        @pl.when(there[way][0])
        def _():
            copy(way, view, slot, k).start()

    def arrive(view, slot, k):
        copy(TWIN, view, slot, k).wait_recv()

    def sides(step, act):
        for sign, onward in ((-1, UP), (1, DOWN)):
            view = v + sign * step

            @pl.when((view >= 0) & (view < views))
            def _():
                act(view, onward)

    for k in range(CHUNKS):
        for way in (UP, DOWN, RIGHT, LEFT, TWIN):
            send(way, v, p, k)

    def along_view(step):
        def act(view, onward):
            for k in range(CHUNKS):
                arrive(view, p, k)
                for way in (onward, RIGHT, LEFT, TWIN):
                    send(way, view, p, k)

        sides(step, act)

    def along_x(view):
        for step in range(1, chips):
            for sign, way in ((-1, RIGHT), (1, LEFT)):
                origin = x + sign * step

                @pl.when((origin >= 0) & (origin < chips))
                def _():
                    slot = 2 * origin + c
                    for k in range(CHUNKS):
                        arrive(view, slot, k)
                        send(way, view, slot, k)
                        send(TWIN, view, slot, k)

    def from_twin(view, q):
        for k in range(CHUNKS):
            arrive(view, 2 * q + 1 - c, k)

    def pair(view, q):
        return held[view, pl.ds(2 * q, 2), :rows, :].reshape(2 * rows, width)

    def exponent(left, right):
        dots = lax.dot_general(
            left, right, (((1,), (1,)), ((), ())), preferred_element_type=jnp.float32
        )
        return dots * (INV_TEMP * LOG2E)

    eye = lax.broadcasted_iota(jnp.int32, (rows, rows), 0) == lax.broadcasted_iota(
        jnp.int32, (rows, rows), 1
    )

    def half(view, place, q):
        from_twin(view, q)
        right = pair(view, q)
        power = exponent(held[v, p, :rows, :], right)
        expo = jnp.exp2(power)
        row_total[place] += jnp.sum(expo, axis=1, keepdims=True)
        mine = match_ref[pl.ds(view, 1), :]
        mine = jnp.sum(jnp.where(eye, mine, 0).astype(jnp.float32), axis=1, keepdims=True)
        first = (2 * q * rows).astype(jnp.float32)
        ids = lax.broadcasted_iota(jnp.int32, expo.shape, 1).astype(jnp.float32) + first
        row_hit = ids == mine
        loss[...] -= (1.0 / LOG2E) * jnp.sum(
            jnp.where(row_hit, power, 0.0), axis=1, keepdims=True
        )

        def add(k, total):
            other = held[v, lax.rem(p + k, slots), :rows, :]
            return total + jnp.sum(jnp.exp2(exponent(other, right)), axis=0, keepdims=True)

        col_total = lax.fori_loop(
            1, slots, add, jnp.sum(expo, axis=0, keepdims=True), unroll=slots <= 4
        )
        at = lax.broadcasted_iota(jnp.int32, (extra, width), 0)
        digit = jnp.where(at == v, 256.0, jnp.where(at == v + views, 1.0, 0.0))
        theirs = [
            jnp.sum(
                digit * held[view, 2 * q + s, rows:, :].astype(jnp.float32), axis=0, keepdims=True
            )[:, :rows]
            for s in range(2)
        ]
        theirs = jnp.concatenate(theirs, axis=1)
        own_ids = (lax.broadcasted_iota(jnp.int32, expo.shape, 0) + p * rows).astype(jnp.float32)
        col_hit = own_ids == theirs
        expos[place, q] = expo
        rest[place, q] = (
            expo * (1.0 / col_total) - jnp.where(row_hit, 1.0, 0.0) - jnp.where(col_hit, 1.0, 0.0)
        )

    def finish(view, place):
        total = row_total[place]
        row_total[place] = jnp.zeros_like(total)
        loss[...] += jnp.log(total)
        inverse = 1.0 / total

        def one(q, carry):
            weight = expos[place, q] * inverse + rest[place, q]
            acc[...] += jnp.dot(
                weight.astype(jnp.bfloat16), pair(view, q), preferred_element_type=jnp.float32
            )
            return carry

        lax.fori_loop(0, chips, one, 0, unroll=chips <= 2)

    row_total[...] = jnp.zeros_like(row_total)

    def round_of(step, carry):
        @pl.when(step < views)
        def _():
            along_view(step)

        @pl.when(step == 1)
        def _():
            along_x(v)
            for q in range(chips):
                from_twin(v, q)

        @pl.when(step > 1)
        def _():
            sides(step - 1, lambda view, onward: along_x(view))

        def work(k, carry):
            late = (k // 2) == 0
            away = jnp.where(late, step - 1, step)
            side = lax.rem(k, 2)
            view = v + away * (2 * side - 1)
            place = 2 * lax.rem(away, 2) + side
            fine = (view >= 0) & (view < views) & (away >= 1) & (away < views)

            def part(n, carry):
                half(view, place, lax.rem(x + n, chips))
                return carry

            @pl.when(fine)
            def _():
                lax.fori_loop(jnp.where(late, 1, 0), jnp.where(late, chips, 1), part, 0)

            @pl.when(fine & late)
            def _():
                finish(view, place)

            return carry

        lax.fori_loop(0, 4, work, 0)
        return carry

    lax.fori_loop(1, views + 1, round_of, 0)

    unit_grad = (INV_TEMP / (views - 1)) * acc[...]
    raw = desc_ref[...].astype(jnp.float32)
    scale = lax.rsqrt(jnp.mean(raw * raw, axis=-1, keepdims=True) + 1e-06) / math.sqrt(width)
    unit = raw * scale
    along = jnp.sum(unit * unit_grad, axis=-1, keepdims=True)
    grad_ref[...] = (scale * (unit_grad - unit * along)).astype(jnp.bfloat16)
    loss_ref[...] = jnp.sum(
        jnp.where(eye, loss[...] * (1.0 / (views - 1)), 0.0), axis=0, keepdims=True
    )

    def sent(way, view, slot):
        @pl.when(there[way][0])
        def _():
            for k in range(CHUNKS):
                copy(way, view, slot, k).wait_send()

    def drain(view, carry):
        @pl.when(view <= v)
        def _():
            sent(UP, view, p)

        @pl.when(view >= v)
        def _():
            sent(DOWN, view, p)

        for q in range(chips):
            slot = 2 * q + c
            sent(TWIN, view, slot)

            @pl.when(q <= x)
            def _():
                sent(RIGHT, view, slot)

            @pl.when(q >= x)
            def _():
                sent(LEFT, view, slot)

        return carry

    lax.fori_loop(0, views, drain, 0)


def body(views, slots, descriptors, matches):
    rows, width = descriptors.shape[1:]
    extra = -(-2 * views // 16) * 16
    grad, loss = pl.pallas_call(
        functools.partial(kernel, views, slots),
        out_shape=(
            jax.ShapeDtypeStruct((rows, width), jnp.bfloat16),
            jax.ShapeDtypeStruct((1, rows), jnp.float32),
        ),
        in_specs=[pl.BlockSpec(memory_space=pltpu.HBM)] * 2,
        out_specs=(pl.BlockSpec(memory_space=pltpu.VMEM),) * 2,
        scratch_shapes=[
            pltpu.VMEM((rows, width), jnp.bfloat16),
            pltpu.VMEM((views, rows), jnp.int32),
            pltpu.VMEM((views, slots, rows + extra, width), jnp.bfloat16),
            pltpu.VMEM((rows, width), jnp.float32),
            pltpu.VMEM((rows, 1), jnp.float32),
            pltpu.VMEM((4, slots // 2, rows, 2 * rows), jnp.float32),
            pltpu.VMEM((4, slots // 2, rows, 2 * rows), jnp.float32),
            pltpu.VMEM((4, rows, 1), jnp.float32),
            pltpu.SemaphoreType.DMA((2,)),
            pltpu.SemaphoreType.DMA((5, views, slots, CHUNKS)),
            pltpu.SemaphoreType.DMA((views, slots, CHUNKS)),
        ],
        compiler_params=pltpu.CompilerParams(
            collective_id=0, has_side_effects=True, vmem_limit_bytes=48 * 1024 * 1024
        ),
        cost_estimate=pl.CostEstimate(
            flops=2 * (slots + 1) * rows * (views - 1) * slots * rows * width,
            bytes_accessed=4 * rows * width,
            transcendentals=slots * rows * (views - 1) * slots * rows,
        ),
    )(descriptors[0], matches[0])
    return grad[None], loss


def solution(mesh):
    views, slots = mesh.shape["view"], mesh.shape["pix"]
    in_specs = (P(("parts", "view"), "pix", None), P(("parts", "view"), None, "pix"))
    out_specs = (P(("parts", "view"), "pix", None), P(("parts", "view"), "pix"))
    return jax.shard_map(
        functools.partial(body, views, slots),
        mesh=mesh, in_specs=in_specs, out_specs=out_specs, check_vma=False,
    )
```

```python
import functools
import math

import jax
import jax.numpy as jnp
from jax import lax
from jax.experimental import pallas as pl
from jax.experimental.pallas import tpu as pltpu
from jax.sharding import PartitionSpec as P

MESH = pl.DeviceIdType.MESH
INV_TEMP = 1.0 / 0.07
LOG2E = math.log2(math.e)
CHUNKS = 2
UP, DOWN, RIGHT, LEFT, TWIN = range(5)


def kernel(
    views, slots, desc_ref, match_ref, grad_ref, loss_ref,
    held, acc, loss, expos, rest, row_total, send_sem, recv_sem,
):
    rows, width = desc_ref.shape
    chips = slots // 2
    extra = held.shape[2] - rows
    tiles = (rows + extra) // 16
    cuts = [16 * (tiles * k // CHUNKS) for k in range(CHUNKS + 1)]
    v = lax.axis_index("view")
    p = lax.axis_index("pix")
    x, c = p // 2, lax.rem(p, 2)
    there = {
        UP: (v + 1 < views, {"view": v + 1}),
        DOWN: (v >= 1, {"view": v - 1}),
        RIGHT: (x + 1 < chips, {"pix": p + 2}),
        LEFT: (x >= 1, {"pix": p - 2}),
        TWIN: (c >= 0, {"pix": p + 1 - 2 * c}),
    }

    barrier = pltpu.get_barrier_semaphore()
    count = 0
    for way in there:
        exists, target = there[way]

        @pl.when(exists)
        def _():
            pl.semaphore_signal(barrier, inc=1, device_id=target, device_id_type=MESH)

        count = count + exists.astype(jnp.int32)

    raw = desc_ref[...].astype(jnp.float32)
    scale = lax.rsqrt(jnp.mean(raw * raw, axis=-1, keepdims=True) + 1e-06) / math.sqrt(width)
    unit = raw * scale
    held[v, p, :rows, :] = unit.astype(jnp.bfloat16)
    own_links = match_ref[...]
    high = own_links // 256
    low = own_links - 256 * high
    links = jnp.concatenate([high, low], axis=0).astype(jnp.float32)
    links = jnp.concatenate([links, jnp.zeros((2 * views, width - rows), jnp.float32)], axis=1)
    if extra > 2 * views:
        links = jnp.concatenate([links, jnp.zeros((extra - 2 * views, width), jnp.float32)], axis=0)
    held[v, p, rows:, :] = links.astype(jnp.bfloat16)
    acc[...] = jnp.zeros_like(acc)
    loss[...] = jnp.zeros_like(loss)
    pl.semaphore_wait(barrier, count)

    def piece(view, slot, k):
        return held.at[view, slot, pl.ds(cuts[k], cuts[k + 1] - cuts[k])]

    def copy(way, view, slot, k):
        return pltpu.make_async_remote_copy(
            src_ref=piece(view, slot, k),
            dst_ref=piece(view, slot, k),
            send_sem=send_sem.at[way, view, slot, k],
            recv_sem=recv_sem.at[view, slot, k],
            device_id=there[way][1],
            device_id_type=MESH,
        )

    def send(way, view, slot, k):
        @pl.when(there[way][0])
        def _():
            copy(way, view, slot, k).start()

    def arrive(view, slot, k):
        copy(TWIN, view, slot, k).wait_recv()

    def sides(step, act):
        for sign, onward in ((-1, UP), (1, DOWN)):
            view = v + sign * step

            @pl.when((view >= 0) & (view < views))
            def _():
                act(view, onward)

    for k in range(CHUNKS):
        for way in (UP, DOWN, RIGHT, LEFT, TWIN):
            send(way, v, p, k)

    def along_view(step):
        def act(view, onward):
            for k in range(CHUNKS):
                arrive(view, p, k)
                for way in (onward, TWIN, RIGHT, LEFT):
                    send(way, view, p, k)

        sides(step, act)

    def along_x(view):
        for step in range(1, chips):
            for sign, way in ((-1, RIGHT), (1, LEFT)):
                origin = x + sign * step

                @pl.when((origin >= 0) & (origin < chips))
                def _():
                    slot = 2 * origin + c
                    for k in range(CHUNKS):
                        arrive(view, slot, k)
                        send(way, view, slot, k)
                        send(TWIN, view, slot, k)

    def from_twin(view, q):
        for k in range(CHUNKS):
            arrive(view, 2 * q + 1 - c, k)

    def pair(view, q):
        return held[view, pl.ds(2 * q, 2), :rows, :].reshape(2 * rows, width)

    def exponent(left, right):
        dots = lax.dot_general(
            left, right, (((1,), (1,)), ((), ())), preferred_element_type=jnp.float32
        )
        return dots * (INV_TEMP * LOG2E)

    eye = lax.broadcasted_iota(jnp.int32, (rows, rows), 0) == lax.broadcasted_iota(
        jnp.int32, (rows, rows), 1
    )

    def half(view, place, q):
        from_twin(view, q)
        right = pair(view, q)
        power = exponent(held[v, p, :rows, :], right)
        expo = jnp.exp2(power)
        row_total[place] += jnp.sum(expo, axis=1, keepdims=True)
        mine = match_ref[pl.ds(view, 1), :]
        mine = jnp.sum(jnp.where(eye, mine, 0).astype(jnp.float32), axis=1, keepdims=True)
        first = (2 * q * rows).astype(jnp.float32)
        ids = lax.broadcasted_iota(jnp.int32, expo.shape, 1).astype(jnp.float32) + first
        row_hit = ids == mine
        loss[...] -= (1.0 / LOG2E) * jnp.sum(
            jnp.where(row_hit, power, 0.0), axis=1, keepdims=True
        )

        def add(k, total):
            other = held[v, lax.rem(p + k, slots), :rows, :]
            return total + jnp.sum(jnp.exp2(exponent(other, right)), axis=0, keepdims=True)

        col_total = lax.fori_loop(
            1, slots, add, jnp.sum(expo, axis=0, keepdims=True), unroll=slots <= 4
        )
        at = lax.broadcasted_iota(jnp.int32, (extra, width), 0)
        digit = jnp.where(at == v, 256.0, jnp.where(at == v + views, 1.0, 0.0))
        theirs = [
            jnp.sum(
                digit * held[view, 2 * q + s, rows:, :].astype(jnp.float32), axis=0, keepdims=True
            )[:, :rows]
            for s in range(2)
        ]
        theirs = jnp.concatenate(theirs, axis=1)
        own_ids = (lax.broadcasted_iota(jnp.int32, expo.shape, 0) + p * rows).astype(jnp.float32)
        col_hit = own_ids == theirs
        expos[place, q] = expo
        rest[place, q] = (
            expo * (1.0 / col_total) - jnp.where(row_hit, 1.0, 0.0) - jnp.where(col_hit, 1.0, 0.0)
        )

    def finish(view, place):
        total = row_total[place]
        row_total[place] = jnp.zeros_like(total)
        loss[...] += jnp.log(total)
        inverse = 1.0 / total

        def one(q, carry):
            weight = expos[place, q] * inverse + rest[place, q]
            acc[...] += jnp.dot(
                weight.astype(jnp.bfloat16), pair(view, q), preferred_element_type=jnp.float32
            )
            return carry

        lax.fori_loop(0, chips, one, 0, unroll=chips <= 2)

    row_total[...] = jnp.zeros_like(row_total)

    def round_of(step, carry):
        @pl.when(step < views)
        def _():
            along_view(step)

        @pl.when(step == 1)
        def _():
            along_x(v)
            for q in range(chips):
                from_twin(v, q)

        @pl.when(step > 1)
        def _():
            sides(step - 1, lambda view, onward: along_x(view))

        def work(k, carry):
            late = (k // 2) == 0
            away = jnp.where(late, step - 1, step)
            side = lax.rem(k, 2)
            view = v + away * (2 * side - 1)
            place = 2 * lax.rem(away, 2) + side
            fine = (view >= 0) & (view < views) & (away >= 1) & (away < views)

            def part(n, carry):
                half(view, place, lax.rem(x + n, chips))
                return carry

            @pl.when(fine)
            def _():
                lax.fori_loop(jnp.where(late, 1, 0), jnp.where(late, chips, 1), part, 0)

            @pl.when(fine & late)
            def _():
                finish(view, place)

            return carry

        lax.fori_loop(0, 4, work, 0)
        return carry

    lax.fori_loop(1, views + 1, round_of, 0)

    unit_grad = (INV_TEMP / (views - 1)) * acc[...]
    raw = desc_ref[...].astype(jnp.float32)
    scale = lax.rsqrt(jnp.mean(raw * raw, axis=-1, keepdims=True) + 1e-06) / math.sqrt(width)
    unit = raw * scale
    along = jnp.sum(unit * unit_grad, axis=-1, keepdims=True)
    grad_ref[...] = (scale * (unit_grad - unit * along)).astype(jnp.bfloat16)
    loss_ref[...] = jnp.sum(
        jnp.where(eye, loss[...] * (1.0 / (views - 1)), 0.0), axis=0, keepdims=True
    )

    def sent(way, view, slot):
        @pl.when(there[way][0])
        def _():
            for k in range(CHUNKS):
                copy(way, view, slot, k).wait_send()

    def drain(view, carry):
        @pl.when(view <= v)
        def _():
            sent(UP, view, p)

        @pl.when(view >= v)
        def _():
            sent(DOWN, view, p)

        for q in range(chips):
            slot = 2 * q + c
            sent(TWIN, view, slot)

            @pl.when(q <= x)
            def _():
                sent(RIGHT, view, slot)

            @pl.when(q >= x)
            def _():
                sent(LEFT, view, slot)

        return carry

    lax.fori_loop(0, views, drain, 0)


def body(views, slots, descriptors, matches):
    rows, width = descriptors.shape[1:]
    extra = -(-2 * views // 16) * 16
    grad, loss = pl.pallas_call(
        functools.partial(kernel, views, slots),
        out_shape=(
            jax.ShapeDtypeStruct((rows, width), jnp.bfloat16),
            jax.ShapeDtypeStruct((1, rows), jnp.float32),
        ),
        in_specs=[pl.BlockSpec(memory_space=pltpu.VMEM)] * 2,
        out_specs=(pl.BlockSpec(memory_space=pltpu.VMEM),) * 2,
        scratch_shapes=[
            pltpu.VMEM((views, slots, rows + extra, width), jnp.bfloat16),
            pltpu.VMEM((rows, width), jnp.float32),
            pltpu.VMEM((rows, 1), jnp.float32),
            pltpu.VMEM((4, slots // 2, rows, 2 * rows), jnp.float32),
            pltpu.VMEM((4, slots // 2, rows, 2 * rows), jnp.float32),
            pltpu.VMEM((4, rows, 1), jnp.float32),
            pltpu.SemaphoreType.DMA((5, views, slots, CHUNKS)),
            pltpu.SemaphoreType.DMA((views, slots, CHUNKS)),
        ],
        compiler_params=pltpu.CompilerParams(
            collective_id=0, has_side_effects=True, vmem_limit_bytes=48 * 1024 * 1024
        ),
        cost_estimate=pl.CostEstimate(
            flops=2 * (slots + 1) * rows * (views - 1) * slots * rows * width,
            bytes_accessed=4 * rows * width,
            transcendentals=slots * rows * (views - 1) * slots * rows,
        ),
    )(descriptors[0], matches[0])
    return grad[None], loss


def solution(mesh):
    views, slots = mesh.shape["view"], mesh.shape["pix"]
    in_specs = (P(("parts", "view"), "pix", None), P(("parts", "view"), None, "pix"))
    out_specs = (P(("parts", "view"), "pix", None), P(("parts", "view"), "pix"))
    return jax.shard_map(
        functools.partial(body, views, slots),
        mesh=mesh, in_specs=in_specs, out_specs=out_specs, check_vma=False,
    )
```
